256 devices in a mesh: seq: 64 (over y, x_lo, z), head: 4 (over x_hi, core).
Axes of the slice: x: 4 (x_hi: 2, x_lo: 2; x = x_hi * 2 + x_lo), y: 4, z: 8, core: 2. Of those that a mesh axis runs over, the one named last changes fastest.
Arguments:
- queries: bfloat16 [4096, 3584], P('seq', 'head')
- key_cache: bfloat16 [40960, 512], P('seq', 'head')
- value_cache: bfloat16 [40960, 512], P('seq', 'head'), may hold values from -6 to 6
- out_weight: bfloat16 [3584, 3584], P('head'), may hold values from -3 to 3
- block_starts: int32 [128], P('seq'), may hold values from 0 to 40928, as said below
- shard_lengths: int32 [64], P('seq'), may hold values from 80 to 640, as said below
Outputs:
- scored: bfloat16 [4096, 3584], P('seq', 'head')
The draws below stay inside these ranges and needn't reach their ends.
Inputs may be any that keep to these rules, and one draw needn't show every extreme that they name: `block_starts`: some block starts at 0 and some at 40928. `shard_lengths`: some shard is full and some holds exactly 80 slots.
All inputs are finite; a program needn't handle non-finite values.
Results may differ from the reference program's by a relative error of at most 0.025.
Values may be sent and summed in bfloat16 or wider, within the bound.
No kernel may reach another device: no remote copies, remote signals or barrier semaphores. Data moves between devices by JAX's collectives and lax.ppermute only.
A program may use at most 128 MiB of HBM per device.

```python
import math
import jax
import jax.numpy as jnp
from jax import lax

D_MODEL = 3584
HEAD_DIM = 128
KVH = 4
QHEADS = 28
BLOCK = 32
S_DEV = 640
SHARDS = 64
CACHE = 40960
NBLK = 128
QTOK = 4096


def draw_queries(key, part):
    key = jax.random.fold_in(key, 11)
    first_key = jax.random.fold_in(key, 0)
    width = QHEADS * HEAD_DIM
    drawn = 2.0 * jax.random.normal(first_key, (QTOK, width), jnp.float32)
    return jnp.clip(drawn, -12.0, 12.0).astype(jnp.bfloat16)


def draw_key_cache(key, part):
    key = jax.random.fold_in(key, 12)
    width = KVH * HEAD_DIM
    drawn = jax.random.normal(key, (CACHE, width), jnp.float32)
    return jnp.clip(drawn, -6.0, 6.0).astype(jnp.bfloat16)


def draw_block_starts(key, part):
    key = jax.random.fold_in(key, 21)
    first_key, second_key, third_key = jax.random.split(key, 3)
    highest = CACHE - BLOCK
    starts = jax.random.randint(first_key, (NBLK,), 0, highest + 1)
    highest_slot = jax.random.randint(second_key, (), 0, NBLK)
    lowest_slot = (highest_slot + 1 + jax.random.randint(third_key, (), 0, NBLK - 1)) % NBLK
    slots = jnp.arange(NBLK)
    starts = jnp.where(slots == highest_slot, highest, starts)
    return jnp.where(slots == lowest_slot, 0, starts).astype(jnp.int32)


def draw_shard_lengths(key, part):
    key = jax.random.fold_in(key, 22)
    first_key, second_key, third_key = jax.random.split(key, 3)
    lowest = S_DEV // 8
    lengths = jax.random.randint(first_key, (SHARDS,), lowest, S_DEV + 1)
    highest_slot = jax.random.randint(second_key, (), 0, SHARDS)
    lowest_slot = (highest_slot + 1 + jax.random.randint(third_key, (), 0, SHARDS - 1)) % SHARDS
    slots = jnp.arange(SHARDS)
    lengths = jnp.where(slots == highest_slot, S_DEV, lengths)
    return jnp.where(slots == lowest_slot, lowest, lengths).astype(jnp.int32)


def strengthened(drawn, own_key, source, target, shards_of, factor):
    def block_of(position):
        return (jnp.arange(drawn.shape[position]) // (drawn.shape[position] // shards_of)).reshape((-1,) + (1,) * (drawn.ndim - 1 - position))

    one_side = jax.random.permutation(own_key, shards_of)[block_of(target)]
    far = (block_of(target) + shards_of // 2) % shards_of
    return jnp.where((block_of(source) == one_side) | (block_of(source) == far), factor * drawn, drawn)


def block_levels(key, shape, shards, least, largest):
    gain = 1.0
    for dim, parts in shards:
        heights = jax.random.uniform(jax.random.fold_in(jax.random.fold_in(key, 6), dim), (parts,), jnp.float32, least / len(shards), largest / len(shards))
        gain = gain * jnp.repeat(jnp.exp(heights), shape[dim] // parts).reshape((-1,) + (1,) * (len(shape) - 1 - dim))
    return gain


def noise(own_key, shape, deviation, most, cuts=(), held_as=jnp.bfloat16):
    values = jax.random.normal(own_key, shape, jnp.float32) * deviation
    if len(cuts) > 0:
        values = block_levels(own_key, shape, cuts, -0.22, 0.18) * values
    return jnp.clip(values, min=-most, max=most).astype(held_as)


def noise_with(stream_key, dims, scale, limit, cuts, heavy, kind=jnp.bfloat16):
    drawn = scale * jax.random.normal(stream_key, dims, jnp.float32)
    if cuts:
        drawn = drawn * block_levels(stream_key, dims, cuts, -0.22, 0.18)
    return jnp.clip(strengthened(drawn, jax.random.fold_in(stream_key, 3), *heavy), -limit, limit).astype(kind)


def setup_inputs(seed: int = 0) -> dict:
    keys = jax.random.split(jax.random.key(seed), 7)
    return {
        "queries": draw_queries(jax.random.fold_in(keys[6], 71), 0),
        "key_cache": draw_key_cache(jax.random.fold_in(keys[6], 71), 0),
        "value_cache": noise(keys[2], (CACHE, KVH * HEAD_DIM), 1.0, 6.0, ((0, 64), (1, 4))),
        "out_weight": noise_with(keys[3], (QHEADS * HEAD_DIM, D_MODEL), 0.5, 3.0, ((0, 4),), (0, 1, 4, 2.0)),
        "block_starts": draw_block_starts(jax.random.fold_in(keys[6], 71), 0),
        "shard_lengths": draw_shard_lengths(jax.random.fold_in(keys[6], 71), 0),
    }


def reference(queries, key_cache, value_cache, out_weight, block_starts, shard_lengths):
    cache_rows = key_cache.shape[0]
    per_kv = QHEADS // KVH
    key_pos = jnp.arange(cache_rows, dtype=jnp.int32)
    key_live = key_pos % S_DEV < jnp.repeat(shard_lengths, S_DEV)
    keys_wide = key_cache.astype(jnp.float32).reshape(cache_rows, KVH, HEAD_DIM)
    values_wide = value_cache.astype(jnp.float32).reshape(cache_rows, KVH, HEAD_DIM)
    score_scale = 1.0 / math.sqrt(HEAD_DIM)

    def one_block(entry):
        query_block, first_pos = entry
        query_wide = query_block.astype(jnp.float32).reshape(BLOCK, KVH, per_kv, HEAD_DIM)
        query_pos = first_pos + jnp.arange(BLOCK, dtype=jnp.int32)
        scores = jnp.einsum('thgd,khd->hgtk', query_wide, keys_wide) * score_scale
        allowed = (key_pos[None, :] <= query_pos[:, None]) & key_live[None, :]
        scores = jnp.where(allowed, scores, -jnp.inf)
        highest = lax.optimization_barrier(jnp.max(scores, axis=3, keepdims=True))
        weights = jnp.exp(scores - highest)
        denominators = lax.optimization_barrier(jnp.sum(weights, axis=3))
        rounded = lax.optimization_barrier(weights.astype(jnp.bfloat16)).astype(jnp.float32)
        numerators = jnp.einsum('hgtk,khd->thgd', rounded, values_wide)
        result = numerators / jnp.transpose(denominators, (2, 0, 1))[..., None]
        return result.reshape(BLOCK, QHEADS * HEAD_DIM).astype(jnp.bfloat16)
    attended = lax.map(one_block, (queries.reshape(-1, BLOCK, QHEADS * HEAD_DIM), block_starts))
    attended = attended.reshape(-1, QHEADS * HEAD_DIM)
    return jnp.dot(attended, out_weight, preferred_element_type=jnp.float32).astype(jnp.bfloat16)
```

```python
import functools
import math

import jax
import jax.numpy as jnp
import numpy as np
from jax import lax
from jax.experimental import pallas as pl
from jax.experimental.pallas import tpu as pltpu
from jax.sharding import PartitionSpec as P

HD = 128
BT = 32
T = 256
TILES = T // 128
G = 4
R = 256
VR = HD + 16
HDR = 16
SCALE = math.log2(math.e) / math.sqrt(HD)
MASKED = -1e30
FLOOR = -1e29
FAR = 2**30
AXES = ("seq", "head")
MIB = 2**20
BF = jnp.bfloat16
F32 = jnp.float32

GRID = np.arange(256).reshape(4, 2, 8, 2, 2)
CYCLE = [(0, 0), (1, 0), (2, 0), (3, 0), (3, 1), (2, 1), (1, 1), (0, 1)]
SKEW = 0


def key_rings():
    found = []
    for g in range(2):
        for y, x in CYCLE:
            found.append(
                [int(GRID[(y + SKEW * (z // 4)) % 4, x, z, g, 0]) for z in range(8)]
            )
        for z in range(8):
            found.append([int(GRID[y, x, z, g, 1]) for y, x in CYCLE])
    return found


def query_groups():
    found = []
    for g in range(2):
        for z in range(8):
            found.append([int(GRID[y, x, z, g, 0]) for y, x in CYCLE])
        for y, x in CYCLE:
            found.append([int(GRID[y, x, z, g, 1]) for z in range(8)])
    return found


KEY_RINGS = key_rings()
QUERY_GROUPS = query_groups()


def swap_even(x):
    return lax.ppermute(x, AXES, [(r[i], r[i ^ 1]) for r in KEY_RINGS for i in range(8)])


def swap_odd(x):
    pairs = [(r[i], r[(i + 1 if i % 2 else i - 1) % 8]) for r in KEY_RINGS for i in range(8)]
    return lax.ppermute(x, AXES, pairs)


def forward(pair):
    return swap_even(pair[1]), swap_odd(pair[0])


def exchange(x):
    return lax.all_to_all(x, AXES, 0, 0, axis_index_groups=QUERY_GROUPS)


def swap_head(x, by):
    pairs = [(d, (d & ~3) | ((d & 3) ^ by)) for d in range(256)]
    return lax.ppermute(x, AXES, pairs)


def vmem():
    return pl.BlockSpec(memory_space=pltpu.VMEM)


def smem():
    return pl.BlockSpec(memory_space=pltpu.SMEM)


def params(mib):
    return pltpu.CompilerParams(vmem_limit_bytes=mib * MIB)


def hbm():
    return pl.BlockSpec(memory_space=pltpu.HBM)


def run_all(copies):
    for copy in copies:
        copy.start()
    for copy in copies:
        copy.wait()


def queries_kernel(starts, q, message, at_s, wide, sems):
    width = q.shape[1]
    copies = [
        pltpu.make_async_copy(starts, at_s, sems.at[0]),
        pltpu.make_async_copy(q, wide.at[:, pl.ds(0, width)], sems.at[1]),
    ]
    for copy in copies:
        copy.start()
    copies[0].wait()
    row = lax.broadcasted_iota(jnp.int32, (64, 128), 0)
    lane = lax.broadcasted_iota(jnp.int32, (64, 128), 1)
    value = jnp.zeros((64, 128), jnp.int32)
    for e in range(2):
        at = at_s[e]
        value = jnp.where((row == 0) & (lane == e), lax.shift_right_logical(at, 8), value)
        value = jnp.where((row == 1) & (lane == e), at & 255, value)
    wide[:, width:] = value.astype(F32).astype(BF)
    copies[1].wait()
    run_all([pltpu.make_async_copy(wide, message.at[a], sems.at[2 + a]) for a in range(8)])


def prepare_queries(starts, q):
    wide = (q.shape[0], q.shape[1] + 128)
    return pl.pallas_call(
        queries_kernel,
        out_shape=jax.ShapeDtypeStruct((8, *wide), BF),
        in_specs=[hbm(), hbm()],
        out_specs=hbm(),
        scratch_shapes=[
            pltpu.SMEM(starts.shape, jnp.int32),
            pltpu.VMEM(wide, BF),
            pltpu.SemaphoreType.DMA((10,)),
        ],
        compiler_params=params(60),
        name="prepare_queries",
    )(starts, q)


def keys_kernel(base, length, k, out, len_s, sems):
    rows = k.shape[0]
    copies = [
        pltpu.make_async_copy(length, len_s, sems.at[0]),
        pltpu.make_async_copy(k, out.at[pl.ds(0, rows)], sems.at[1]),
    ]
    for copy in copies:
        copy.start()
    copies[0].wait()
    row = lax.broadcasted_iota(jnp.int32, (HDR, HD), 0)
    value = jnp.where(row == 0, lax.shift_right_logical(base[0], 8), base[0] & 255)
    value = jnp.where(row == 2, lax.shift_right_logical(len_s[0], 3), value)
    value = jnp.where(row == 3, len_s[0] & 7, value)
    out[rows:, :] = value.astype(F32).astype(BF)
    copies[1].wait()


def prepare_keys(base, length, k):
    return pl.pallas_call(
        keys_kernel,
        out_shape=jax.ShapeDtypeStruct((k.shape[0] + HDR, HD), BF),
        in_specs=[smem(), hbm(), hbm()],
        out_specs=vmem(),
        scratch_shapes=[
            pltpu.SMEM(length.shape, jnp.int32),
            pltpu.SemaphoreType.DMA((2,)),
        ],
        compiler_params=params(60),
        name="prepare_keys",
    )(base, length, k)


def attend_shards(info, kvs, qb, acc, m, s):
    nb = 16
    rows = kvs[0][1].shape[0]
    tiles = rows // 128
    most = chunks_of(len(kvs) * rows)
    second = most * nb + 4 * G
    heads = []
    for k, _ in kvs:
        h = k[rows:, :].astype(F32)
        base = (h[0:1] * 256.0 + h[1:2]).astype(jnp.int32)
        length = (h[2:3] * 8.0 + h[3:4]).astype(jnp.int32)
        heads.append((base[0, 0], length[0, 0]))

    sub = lax.broadcasted_iota(jnp.int32, (128, 128), 0)
    ones = jnp.ones((VR - HD, 128), BF)
    for c in range(most + 1):
        s.first[c] = FAR
        s.last[c] = -1

    def place(o, k, v, pos):
        c = lax.div(o, TILES)
        r = pl.multiple_of((o - c * TILES) * 128, 128)
        s.keys[c, pl.ds(r, 128), :] = k
        s.values[c, :HD, pl.ds(r, 128)] = v
        s.values[c, HD:, pl.ds(r, 128)] = ones
        s.pos[c, pl.ds(r, 128), :] = pos
        return c

    off = jnp.int32(0)
    for (k, v), (base, length) in zip(kvs, heads, strict=True):
        for t in range(tiles):

            @pl.when(t * 128 < length)
            def _(t=t, off=off, k=k, v=v, base=base, length=length):
                cut = slice(t * 128, (t + 1) * 128)
                pos = jnp.where(sub + t * 128 < length, sub + (base + t * 128), FAR)
                c = place(off + t, k[cut, :], v[cut, :].T, pos)
                s.first[c] = jnp.minimum(s.first[c], base + t * 128)
                end = jnp.where(t * 128 + 128 <= length, base + t * 128 + 127, FAR)
                s.last[c] = jnp.maximum(s.last[c], end)

        off = off + lax.shift_right_logical(length + 127, 7)
    chunks = lax.div(off + TILES - 1, TILES)

    @pl.when(off < chunks * TILES)
    def _():
        c = place(
            off,
            jnp.zeros((128, HD), BF),
            jnp.zeros((HD, 128), BF),
            jnp.full((128, 128), FAR, jnp.int32),
        )
        s.last[c] = FAR

    def per_chunk(c, count):
        lo, hi = s.first[c], s.last[c]

        def per_block(i, count):
            whole, part = count
            at = info[lax.shift_right_logical(i, 1), i & 1]
            is_whole = at >= hi
            is_part = jnp.logical_not(is_whole) & (at + (BT - 1) >= lo)
            s.items[whole] = c * 32 + i
            s.items[second + part] = c * 32 + i
            return whole + is_whole.astype(jnp.int32), part + is_part.astype(jnp.int32)

        whole, part = lax.fori_loop(0, nb, per_block, count, unroll=True)
        for e in range(G - 1):
            s.items[whole + e] = c * 32 + nb
            s.items[second + part + e] = c * 32 + nb
        return lax.div(whole + G - 1, G) * G, lax.div(part + G - 1, G) * G

    whole, part = lax.fori_loop(0, chunks, per_chunk, (jnp.int32(0), jnp.int32(0)))
    for e in range(3 * G):
        s.items[whole + e] = nb
        s.items[second + part + e] = nb

    def score(at, out):
        for e in range(G):
            it = s.items[at + e]
            out[e] = lax.dot_general(
                s.keys[lax.shift_right_logical(it, 5)],
                qb[it & 31],
                (((1,), (1,)), ((), ())),
                preferred_element_type=F32,
            )

    def update(at, score_ref, masked):
        its = [s.items[at + e] for e in range(G)]
        chunk = [lax.shift_right_logical(it, 5) for it in its]
        block = [it & 31 for it in its]
        before = [m[i] for i in block]
        after = []
        for e in range(G):
            if masked:
                i = jnp.minimum(block[e], nb - 1)
                token = lax.broadcasted_iota(jnp.int32, (1, 128), 1) & (BT - 1)
                pos = token + info[lax.shift_right_logical(i, 1), i & 1]
                ok = s.pos[chunk[e]] <= pos
                score_ref[e] = jnp.where(jnp.concatenate([ok, ok], axis=1), score_ref[e], MASKED)
            after.append(
                jnp.maximum(before[e], jnp.max(score_ref[e], axis=0, keepdims=True) * SCALE)
            )
        for e in range(G):
            m[block[e]] = after[e]
        added = []
        for e in range(G):
            p = jnp.exp2(score_ref[e] * SCALE - after[e]).astype(BF)
            added.append(jnp.dot(s.values[chunk[e]], p, preferred_element_type=F32))
        for e in range(G):
            acc[block[e]] = acc[block[e]] * jnp.exp2(before[e] - after[e]) + added[e]

    def run(begin, count, masked):
        @pl.when(count > 0)
        def _():
            score(begin, s.scores_a)

            def body(g, _):
                at = begin + g * (2 * G)
                score(at + G, s.scores_b)
                update(at, s.scores_a, masked)
                score(at + 2 * G, s.scores_a)
                update(at + G, s.scores_b, masked)
                return 0

            lax.fori_loop(0, lax.div(count + 2 * G - 1, 2 * G), body, 0)

    run(0, whole, False)
    run(second, part, True)


def chunks_of(rows):
    return (rows // 128 + TILES - 1) // TILES


class Scratch:
    NAMES = (
        "items",
        "first",
        "last",
        "keys",
        "values",
        "pos",
        "scores_a",
        "scores_b",
    )

    def __init__(self, refs):
        for name, ref in zip(self.NAMES, refs, strict=True):
            setattr(self, name, ref)

    @staticmethod
    def shapes(rows):
        nb, most = 16, chunks_of(rows)
        return [
            pltpu.SMEM((2 * (most * nb + 8 * G),), jnp.int32),
            pltpu.SMEM((most + 1,), jnp.int32),
            pltpu.SMEM((most + 1,), jnp.int32),
            pltpu.VMEM((most + 1, T, HD), BF),
            pltpu.VMEM((most + 1, VR, T), BF),
            pltpu.VMEM((most + 1, T, 128), jnp.int32),
            pltpu.VMEM((G, T, R), F32),
            pltpu.VMEM((G, T, R), F32),
        ]


def pairs(refs):
    return list(zip(refs[0::2], refs[1::2], strict=True))


def begin(queries, info, qb, acc, m, head, sem):
    width = queries.shape[2] - 128
    for a in range(8):
        h = queries[a, :16, width:].astype(F32)
        head[a : a + 1, :] = (h[0:1] * 256.0 + h[1:2]).astype(jnp.int32)
    copy = pltpu.make_async_copy(head, info, sem)
    copy.start()
    heads = width // HD
    for i in range(16):
        for h in range(heads):
            qb[i, h * BT : (h + 1) * BT, :] = queries[
                i // 2, (i % 2) * BT : (i % 2 + 1) * BT, h * HD : (h + 1) * HD
            ]
        qb[i, heads * BT :, :] = jnp.zeros((R - heads * BT, HD), BF)
    qb[16] = jnp.zeros((R, HD), BF)
    acc[...] = jnp.zeros(acc.shape, F32)
    m[...] = jnp.full(m.shape, FLOOR, F32)
    copy.wait()


def cost(shards):
    return pl.CostEstimate(
        flops=shards * 16 * 256 * 640 * 128 * 4, bytes_accessed=MIB, transcendentals=0
    )


def first_kernel(shards, queries, *refs):
    info, qb, acc, m, head, sem, *scratch = refs[2 * shards :]
    begin(queries, info, qb, acc, m, head, sem)
    attend_shards(info, pairs(refs[: 2 * shards]), qb, acc, m, Scratch(scratch))


def attend_first(queries, kvs):
    shards = len(kvs)
    return pl.pallas_call(
        functools.partial(first_kernel, shards),
        out_shape=(
            jax.ShapeDtypeStruct((8, 128), jnp.int32),
            jax.ShapeDtypeStruct((17, R, HD), BF),
            jax.ShapeDtypeStruct((17, VR, R), F32),
            jax.ShapeDtypeStruct((17, 1, R), F32),
        ),
        in_specs=[vmem()] * (1 + 2 * shards),
        out_specs=(smem(), vmem(), vmem(), vmem()),
        scratch_shapes=[pltpu.VMEM((8, 128), jnp.int32), pltpu.SemaphoreType.DMA]
        + Scratch.shapes(shards * kvs[0][1].shape[0]),
        compiler_params=params(16),
        cost_estimate=cost(shards),
        name="attend_first",
    )(queries, *[x for kv in kvs for x in kv])


def last_kernel(shards, info, qb, acc_in, m_in, *refs):
    out, acc, m, *scratch = refs[2 * shards :]
    attend_shards(info, pairs(refs[: 2 * shards]), qb, acc, m, Scratch(scratch))
    conclude(acc, m, out)


def attend_last(info, qb, acc, m, kvs, width):
    shards = len(kvs)
    out, _, _ = pl.pallas_call(
        functools.partial(last_kernel, shards),
        out_shape=(
            jax.ShapeDtypeStruct((8, 2 * BT, width + 128), BF),
            jax.ShapeDtypeStruct(acc.shape, F32),
            jax.ShapeDtypeStruct(m.shape, F32),
        ),
        in_specs=[smem()] + [vmem()] * (3 + 2 * shards),
        out_specs=(vmem(),) * 3,
        scratch_shapes=Scratch.shapes(shards * kvs[0][1].shape[0]),
        input_output_aliases={2: 1, 3: 2},
        compiler_params=params(16),
        cost_estimate=cost(shards),
        name="attend_last",
    )(info, qb, acc, m, *[x for kv in kvs for x in kv])
    return out


def whole_kernel(shards, queries, *refs):
    out, info, qb, acc, m, head, sem, *scratch = refs[2 * shards :]
    begin(queries, info, qb, acc, m, head, sem)
    attend_shards(info, pairs(refs[: 2 * shards]), qb, acc, m, Scratch(scratch))
    conclude(acc, m, out)


def attend(queries, kvs):
    shards = len(kvs)
    return pl.pallas_call(
        functools.partial(whole_kernel, shards),
        out_shape=jax.ShapeDtypeStruct(queries.shape, BF),
        in_specs=[vmem()] * (1 + 2 * shards),
        out_specs=vmem(),
        scratch_shapes=[
            pltpu.SMEM((8, 128), jnp.int32),
            pltpu.VMEM((17, R, HD), BF),
            pltpu.VMEM((17, VR, R), F32),
            pltpu.VMEM((17, 1, R), F32),
            pltpu.VMEM((8, 128), jnp.int32),
            pltpu.SemaphoreType.DMA,
        ]
        + Scratch.shapes(shards * kvs[0][1].shape[0]),
        compiler_params=params(24),
        cost_estimate=cost(shards),
        name="attend",
    )(queries, *[x for kv in kvs for x in kv])


def conclude(acc, m, out):
    heads = out.shape[2] // HD - 1

    def finish(a, _):
        stats = []
        for b in range(2):
            i = 2 * a + b
            total = acc[i, HD : HD + 1, :]
            some = total > 0.0
            o = acc[i, :HD, :] * jnp.where(some, 1.0 / jnp.where(some, total, 1.0), 0.0)
            o = o.astype(BF).T
            for h in range(heads):
                out[a, b * BT : (b + 1) * BT, h * HD : (h + 1) * HD] = o[h * BT : (h + 1) * BT]
            lse = jnp.where(some, m[i] + jnp.log2(jnp.where(some, total, 1.0)), MASKED)
            for _ in range(3):
                part = lse.astype(BF).astype(F32)
                stats.append(part)
                lse = lse - part
        stats = jnp.concatenate(stats + [jnp.zeros((HDR - 6, R), F32)], axis=0).astype(BF)
        out[a, :HDR, heads * HD :] = stats[:, :128]
        out[a, HDR : 2 * HDR, heads * HD :] = stats[:, 128:]
        out[a, 2 * HDR :, heads * HD :] = jnp.zeros((2 * BT - 2 * HDR, 128), BF)
        return 0

    lax.fori_loop(0, 8, finish, 0, unroll=4)


def merge_kernel(head, parts, weight, own, far, sibling, attended):
    width = own.shape[1]
    cuts = [pl.ds(pl.multiple_of((head[0] ^ by) * width, 128), width) for by in range(4)]
    heads = parts.shape[2] // HD - 1
    for b in range(2):
        stats = []
        for a in range(8):
            x = [parts[a, r : r + HDR, heads * HD :] for r in (0, HDR)]
            x = jnp.concatenate(x, axis=1).astype(F32)
            stats.append(x[3 * b : 3 * b + 1] + x[3 * b + 1 : 3 * b + 2] + x[3 * b + 2 : 3 * b + 3])
        stats = jnp.concatenate(stats, axis=0)
        share = jnp.exp2(stats - jnp.max(stats, axis=0, keepdims=True))
        share = share / jnp.sum(share, axis=0, keepdims=True)
        share = share.T
        for h in range(heads):
            total = jnp.zeros((BT, HD), F32)
            for a in range(8):
                x = parts[a, b * BT : (b + 1) * BT, h * HD : (h + 1) * HD].astype(F32)
                total = total + share[h * BT : (h + 1) * BT, a : a + 1] * x
            attended[b * BT : (b + 1) * BT, h * HD : (h + 1) * HD] = total.astype(BF)
    for by, out in ((1, sibling.at[:, :width]), (3, sibling.at[:, width:]), (2, far), (0, own)):
        x = jnp.dot(attended[...], weight[:, cuts[by]], preferred_element_type=F32)
        out[...] = x.astype(out.dtype)


def merge(head, parts, weight):
    tokens, width = parts.shape[1], parts.shape[2] - 128
    return pl.pallas_call(
        merge_kernel,
        out_shape=(
            jax.ShapeDtypeStruct((tokens, width), F32),
            jax.ShapeDtypeStruct((tokens, width), F32),
            jax.ShapeDtypeStruct((tokens, 2 * width), BF),
        ),
        in_specs=[smem(), vmem(), vmem()],
        out_specs=(vmem(),) * 3,
        scratch_shapes=[pltpu.VMEM((tokens, width), BF)],
        compiler_params=params(16),
        name="merge",
    )(head, parts, weight)


def local(queries, key_cache, value_cache, out_weight, block_starts, shard_lengths):
    width = queries.shape[1]
    base = (lax.axis_index("seq") * key_cache.shape[0]).astype(jnp.int32).reshape(1)
    head = lax.axis_index("head").astype(jnp.int32).reshape(1)
    message = prepare_queries(block_starts, queries)
    keys = prepare_keys(base, shard_lengths, key_cache)

    gathered = exchange(message)
    k1, v1 = forward((keys, keys)), forward((value_cache, value_cache))
    k2, v2 = forward(k1), forward(v1)
    k3, v3 = forward(k2), forward(v2)
    k4, v4 = swap_even(k3[1]), swap_odd(v3[0])
    kvs = [(keys, value_cache), *zip(k1, v1), *zip(k2, v2), *zip(k3, v3), (k4, v4)]
    state = attend_first(gathered, kvs[:5])
    parts = attend_last(*state, kvs[5:], width)

    parts = exchange(parts)
    own, far, sibling = merge(head, parts, out_weight)
    sibling = swap_head(sibling, 1).astype(F32)
    far = swap_head((far + sibling[:, width:]).astype(BF), 2)
    return (own + sibling[:, :width] + far.astype(F32)).astype(BF)


def solution(mesh):
    placed = (
        P("seq", "head"),
        P("seq", "head"),
        P("seq", "head"),
        P("head", None),
        P("seq"),
        P("seq"),
    )
    return jax.shard_map(
        local, mesh=mesh, in_specs=placed, out_specs=P("seq", "head"), check_vma=False
    )
```

```python
import functools
import math

import jax
import jax.numpy as jnp
import numpy as np
from jax import lax
from jax.experimental import pallas as pl
from jax.experimental.pallas import tpu as pltpu
from jax.sharding import PartitionSpec as P

HD = 128
BT = 32
T = 256
TILES = T // 128
G = 4
R = 256
VR = HD + 16
HDR = 16
SCALE = math.log2(math.e) / math.sqrt(HD)
MASKED = -1e30
FLOOR = -1e29
FAR = 2**30
AXES = ("seq", "head")
MIB = 2**20
BF = jnp.bfloat16
F32 = jnp.float32

GRID = np.arange(256).reshape(4, 2, 8, 2, 2)
CYCLE = [(0, 0), (1, 0), (2, 0), (3, 0), (3, 1), (2, 1), (1, 1), (0, 1)]
SKEW = 0


def key_rings():
    found = []
    for g in range(2):
        for y, x in CYCLE:
            found.append(
                [int(GRID[(y + SKEW * (z // 4)) % 4, x, z, g, 0]) for z in range(8)]
            )
        for z in range(8):
            found.append([int(GRID[y, x, z, g, 1]) for y, x in CYCLE])
    return found


def query_groups():
    found = []
    for g in range(2):
        for z in range(8):
            found.append([int(GRID[y, x, z, g, 0]) for y, x in CYCLE])
        for y, x in CYCLE:
            found.append([int(GRID[y, x, z, g, 1]) for z in range(8)])
    return found


KEY_RINGS = key_rings()
QUERY_GROUPS = query_groups()


def swap_even(x):
    return lax.ppermute(x, AXES, [(r[i], r[i ^ 1]) for r in KEY_RINGS for i in range(8)])


def swap_odd(x):
    pairs = [(r[i], r[(i + 1 if i % 2 else i - 1) % 8]) for r in KEY_RINGS for i in range(8)]
    return lax.ppermute(x, AXES, pairs)


def forward(pair):
    return swap_even(pair[1]), swap_odd(pair[0])


def exchange(x):
    return lax.all_to_all(x, AXES, 0, 0, axis_index_groups=QUERY_GROUPS)


def swap_head(x, by):
    pairs = [(d, (d & ~3) | ((d & 3) ^ by)) for d in range(256)]
    return lax.ppermute(x, AXES, pairs)


def vmem():
    return pl.BlockSpec(memory_space=pltpu.VMEM)


def smem():
    return pl.BlockSpec(memory_space=pltpu.SMEM)


def params(mib):
    return pltpu.CompilerParams(vmem_limit_bytes=mib * MIB)


def hbm():
    return pl.BlockSpec(memory_space=pltpu.HBM)


def run_all(copies):
    for copy in copies:
        copy.start()
    for copy in copies:
        copy.wait()


def queries_kernel(starts, q, message, at_s, wide, sems):
    width = q.shape[1]
    copies = [
        pltpu.make_async_copy(starts, at_s, sems.at[0]),
        pltpu.make_async_copy(q, wide.at[:, pl.ds(0, width)], sems.at[1]),
    ]
    for copy in copies:
        copy.start()
    copies[0].wait()
    row = lax.broadcasted_iota(jnp.int32, (64, 128), 0)
    lane = lax.broadcasted_iota(jnp.int32, (64, 128), 1)
    value = jnp.zeros((64, 128), jnp.int32)
    for e in range(2):
        at = at_s[e]
        value = jnp.where((row == 0) & (lane == e), lax.shift_right_logical(at, 8), value)
        value = jnp.where((row == 1) & (lane == e), at & 255, value)
    wide[:, width:] = value.astype(F32).astype(BF)
    copies[1].wait()
    run_all([pltpu.make_async_copy(wide, message.at[a], sems.at[2 + a]) for a in range(8)])


def prepare_queries(starts, q):
    wide = (q.shape[0], q.shape[1] + 128)
    return pl.pallas_call(
        queries_kernel,
        out_shape=jax.ShapeDtypeStruct((8, *wide), BF),
        in_specs=[hbm(), hbm()],
        out_specs=hbm(),
        scratch_shapes=[
            pltpu.SMEM(starts.shape, jnp.int32),
            pltpu.VMEM(wide, BF),
            pltpu.SemaphoreType.DMA((10,)),
        ],
        compiler_params=params(60),
        name="prepare_queries",
    )(starts, q)


def keys_kernel(base, length, k, out, len_s, sems):
    rows = k.shape[0]
    copies = [
        pltpu.make_async_copy(length, len_s, sems.at[0]),
        pltpu.make_async_copy(k, out.at[pl.ds(0, rows)], sems.at[1]),
    ]
    for copy in copies:
        copy.start()
    copies[0].wait()
    row = lax.broadcasted_iota(jnp.int32, (HDR, HD), 0)
    value = jnp.where(row == 0, lax.shift_right_logical(base[0], 8), base[0] & 255)
    value = jnp.where(row == 2, lax.shift_right_logical(len_s[0], 3), value)
    value = jnp.where(row == 3, len_s[0] & 7, value)
    out[rows:, :] = value.astype(F32).astype(BF)
    copies[1].wait()


def prepare_keys(base, length, k):
    return pl.pallas_call(
        keys_kernel,
        out_shape=jax.ShapeDtypeStruct((k.shape[0] + HDR, HD), BF),
        in_specs=[smem(), hbm(), hbm()],
        out_specs=vmem(),
        scratch_shapes=[
            pltpu.SMEM(length.shape, jnp.int32),
            pltpu.SemaphoreType.DMA((2,)),
        ],
        compiler_params=params(60),
        name="prepare_keys",
    )(base, length, k)


def attend_shards(info, kvs, qb, acc, m, s):
    nb = 16
    rows = kvs[0][1].shape[0]
    tiles = rows // 128
    most = chunks_of(len(kvs) * rows)
    second = most * nb + 4 * G
    heads = []
    for k, _ in kvs:
        h = k[rows:, :].astype(F32)
        base = (h[0:1] * 256.0 + h[1:2]).astype(jnp.int32)
        length = (h[2:3] * 8.0 + h[3:4]).astype(jnp.int32)
        heads.append((base[0, 0], length[0, 0]))

    sub = lax.broadcasted_iota(jnp.int32, (128, 128), 0)
    ones = jnp.ones((VR - HD, 128), BF)
    for c in range(most + 1):
        s.first[c] = FAR
        s.last[c] = -1

    def place(o, k, v, pos):
        c = lax.div(o, TILES)
        r = pl.multiple_of((o - c * TILES) * 128, 128)
        s.keys[c, pl.ds(r, 128), :] = k
        s.values[c, :HD, pl.ds(r, 128)] = v
        s.values[c, HD:, pl.ds(r, 128)] = ones
        s.pos[c, pl.ds(r, 128), :] = pos
        return c

    off = jnp.int32(0)
    for (k, v), (base, length) in zip(kvs, heads, strict=True):
        for t in range(tiles):

            @pl.when(t * 128 < length)
            def _(t=t, off=off, k=k, v=v, base=base, length=length):
                cut = slice(t * 128, (t + 1) * 128)
                pos = jnp.where(sub + t * 128 < length, sub + (base + t * 128), FAR)
                c = place(off + t, k[cut, :], v[cut, :].T, pos)
                s.first[c] = jnp.minimum(s.first[c], base + t * 128)
                end = jnp.where(t * 128 + 128 <= length, base + t * 128 + 127, FAR)
                s.last[c] = jnp.maximum(s.last[c], end)

        off = off + lax.shift_right_logical(length + 127, 7)
    chunks = lax.div(off + TILES - 1, TILES)

    @pl.when(off < chunks * TILES)
    def _():
        c = place(
            off,
            jnp.zeros((128, HD), BF),
            jnp.zeros((HD, 128), BF),
            jnp.full((128, 128), FAR, jnp.int32),
        )
        s.last[c] = FAR

    def per_chunk(c, count):
        lo, hi = s.first[c], s.last[c]

        def per_block(i, count):
            whole, part = count
            at = info[lax.shift_right_logical(i, 1), i & 1]
            is_whole = at >= hi
            is_part = jnp.logical_not(is_whole) & (at + (BT - 1) >= lo)
            s.items[whole] = c * 32 + i
            s.items[second + part] = c * 32 + i
            return whole + is_whole.astype(jnp.int32), part + is_part.astype(jnp.int32)

        whole, part = lax.fori_loop(0, nb, per_block, count, unroll=True)
        for e in range(G - 1):
            s.items[whole + e] = c * 32 + nb
            s.items[second + part + e] = c * 32 + nb
        return lax.div(whole + G - 1, G) * G, lax.div(part + G - 1, G) * G

    whole, part = lax.fori_loop(0, chunks, per_chunk, (jnp.int32(0), jnp.int32(0)))
    for e in range(3 * G):
        s.items[whole + e] = nb
        s.items[second + part + e] = nb

    def score(at, out):
        for e in range(G):
            it = s.items[at + e]
            out[e] = lax.dot_general(
                s.keys[lax.shift_right_logical(it, 5)],
                qb[it & 31],
                (((1,), (1,)), ((), ())),
                preferred_element_type=F32,
            )

    def update(at, score_ref, masked):
        its = [s.items[at + e] for e in range(G)]
        chunk = [lax.shift_right_logical(it, 5) for it in its]
        block = [it & 31 for it in its]
        before = [m[i] for i in block]
        after = []
        for e in range(G):
            if masked:
                i = jnp.minimum(block[e], nb - 1)
                token = lax.broadcasted_iota(jnp.int32, (1, 128), 1) & (BT - 1)
                pos = token + info[lax.shift_right_logical(i, 1), i & 1]
                ok = s.pos[chunk[e]] <= pos
                score_ref[e] = jnp.where(jnp.concatenate([ok, ok], axis=1), score_ref[e], MASKED)
            after.append(
                jnp.maximum(before[e], jnp.max(score_ref[e], axis=0, keepdims=True) * SCALE)
            )
        for e in range(G):
            m[block[e]] = after[e]
        added = []
        for e in range(G):
            p = jnp.exp2(score_ref[e] * SCALE - after[e]).astype(BF)
            added.append(jnp.dot(s.values[chunk[e]], p, preferred_element_type=F32))
        for e in range(G):
            acc[block[e]] = acc[block[e]] * jnp.exp2(before[e] - after[e]) + added[e]

    def run(begin, count, masked):
        @pl.when(count > 0)
        def _():
            score(begin, s.scores_a)

            def body(g, _):
                at = begin + g * (2 * G)
                score(at + G, s.scores_b)
                update(at, s.scores_a, masked)
                score(at + 2 * G, s.scores_a)
                update(at + G, s.scores_b, masked)
                return 0

            lax.fori_loop(0, lax.div(count + 2 * G - 1, 2 * G), body, 0)

    run(0, whole, False)
    run(second, part, True)


def chunks_of(rows):
    return (rows // 128 + TILES - 1) // TILES


class Scratch:
    NAMES = (
        "items",
        "first",
        "last",
        "keys",
        "values",
        "pos",
        "scores_a",
        "scores_b",
    )

    def __init__(self, refs):
        for name, ref in zip(self.NAMES, refs, strict=True):
            setattr(self, name, ref)

    @staticmethod
    def shapes(rows):
        nb, most = 16, chunks_of(rows)
        return [
            pltpu.SMEM((2 * (most * nb + 8 * G),), jnp.int32),
            pltpu.SMEM((most + 1,), jnp.int32),
            pltpu.SMEM((most + 1,), jnp.int32),
            pltpu.VMEM((most + 1, T, HD), BF),
            pltpu.VMEM((most + 1, VR, T), BF),
            pltpu.VMEM((most + 1, T, 128), jnp.int32),
            pltpu.VMEM((G, T, R), F32),
            pltpu.VMEM((G, T, R), F32),
        ]


def pairs(refs):
    return list(zip(refs[0::2], refs[1::2], strict=True))


def begin(queries, info, qb, acc, m, head, sem):
    width = queries.shape[2] - 128
    for a in range(8):
        h = queries[a, :16, width:].astype(F32)
        head[a : a + 1, :] = (h[0:1] * 256.0 + h[1:2]).astype(jnp.int32)
    copy = pltpu.make_async_copy(head, info, sem)
    copy.start()
    heads = width // HD
    for i in range(16):
        for h in range(heads):
            qb[i, h * BT : (h + 1) * BT, :] = queries[
                i // 2, (i % 2) * BT : (i % 2 + 1) * BT, h * HD : (h + 1) * HD
            ]
        qb[i, heads * BT :, :] = jnp.zeros((R - heads * BT, HD), BF)
    qb[16] = jnp.zeros((R, HD), BF)
    acc[...] = jnp.zeros(acc.shape, F32)
    m[...] = jnp.full(m.shape, FLOOR, F32)
    copy.wait()


def cost(shards):
    return pl.CostEstimate(
        flops=shards * 16 * 256 * 640 * 128 * 4, bytes_accessed=MIB, transcendentals=0
    )


def first_kernel(shards, queries, *refs):
    info, qb, acc, m, head, sem, *scratch = refs[2 * shards :]
    begin(queries, info, qb, acc, m, head, sem)
    attend_shards(info, pairs(refs[: 2 * shards]), qb, acc, m, Scratch(scratch))


def attend_first(queries, kvs):
    shards = len(kvs)
    return pl.pallas_call(
        functools.partial(first_kernel, shards),
        out_shape=(
            jax.ShapeDtypeStruct((8, 128), jnp.int32),
            jax.ShapeDtypeStruct((17, R, HD), BF),
            jax.ShapeDtypeStruct((17, VR, R), F32),
            jax.ShapeDtypeStruct((17, 1, R), F32),
        ),
        in_specs=[vmem()] * (1 + 2 * shards),
        out_specs=(smem(), vmem(), vmem(), vmem()),
        scratch_shapes=[pltpu.VMEM((8, 128), jnp.int32), pltpu.SemaphoreType.DMA]
        + Scratch.shapes(shards * kvs[0][1].shape[0]),
        compiler_params=params(16),
        cost_estimate=cost(shards),
        name="attend_first",
    )(queries, *[x for kv in kvs for x in kv])


def last_kernel(shards, info, qb, acc_in, m_in, *refs):
    out, acc, m, *scratch = refs[2 * shards :]
    attend_shards(info, pairs(refs[: 2 * shards]), qb, acc, m, Scratch(scratch))
    conclude(acc, m, out)


def attend_last(info, qb, acc, m, kvs, width):
    shards = len(kvs)
    out, _, _ = pl.pallas_call(
        functools.partial(last_kernel, shards),
        out_shape=(
            jax.ShapeDtypeStruct((8, 2 * BT, width + 128), BF),
            jax.ShapeDtypeStruct(acc.shape, F32),
            jax.ShapeDtypeStruct(m.shape, F32),
        ),
        in_specs=[smem()] + [vmem()] * (3 + 2 * shards),
        out_specs=(vmem(),) * 3,
        scratch_shapes=Scratch.shapes(shards * kvs[0][1].shape[0]),
        input_output_aliases={2: 1, 3: 2},
        compiler_params=params(16),
        cost_estimate=cost(shards),
        name="attend_last",
    )(info, qb, acc, m, *[x for kv in kvs for x in kv])
    return out


def whole_kernel(shards, queries, *refs):
    out, info, qb, acc, m, head, sem, *scratch = refs[2 * shards :]
    begin(queries, info, qb, acc, m, head, sem)
    attend_shards(info, pairs(refs[: 2 * shards]), qb, acc, m, Scratch(scratch))
    conclude(acc, m, out)


def attend(queries, kvs):
    shards = len(kvs)
    return pl.pallas_call(
        functools.partial(whole_kernel, shards),
        out_shape=jax.ShapeDtypeStruct(queries.shape, BF),
        in_specs=[vmem()] * (1 + 2 * shards),
        out_specs=vmem(),
        scratch_shapes=[
            pltpu.SMEM((8, 128), jnp.int32),
            pltpu.VMEM((17, R, HD), BF),
            pltpu.VMEM((17, VR, R), F32),
            pltpu.VMEM((17, 1, R), F32),
            pltpu.VMEM((8, 128), jnp.int32),
            pltpu.SemaphoreType.DMA,
        ]
        + Scratch.shapes(shards * kvs[0][1].shape[0]),
        compiler_params=params(24),
        cost_estimate=cost(shards),
        name="attend",
    )(queries, *[x for kv in kvs for x in kv])


def conclude(acc, m, out):
    heads = out.shape[2] // HD - 1

    def finish(a, _):
        stats = []
        for b in range(2):
            i = 2 * a + b
            total = acc[i, HD : HD + 1, :]
            some = total > 0.0
            o = acc[i, :HD, :] * jnp.where(some, 1.0 / jnp.where(some, total, 1.0), 0.0)
            o = o.astype(BF).T
            for h in range(heads):
                out[a, b * BT : (b + 1) * BT, h * HD : (h + 1) * HD] = o[h * BT : (h + 1) * BT]
            lse = jnp.where(some, m[i] + jnp.log2(jnp.where(some, total, 1.0)), MASKED)
            for _ in range(3):
                part = lse.astype(BF).astype(F32)
                stats.append(part)
                lse = lse - part
        stats = jnp.concatenate(stats + [jnp.zeros((HDR - 6, R), F32)], axis=0).astype(BF)
        out[a, :HDR, heads * HD :] = stats[:, :128]
        out[a, HDR : 2 * HDR, heads * HD :] = stats[:, 128:]
        out[a, 2 * HDR :, heads * HD :] = jnp.zeros((2 * BT - 2 * HDR, 128), BF)
        return 0

    lax.fori_loop(0, 8, finish, 0, unroll=4)


def merge_kernel(head, parts, weight, own, far, sibling, attended, held, total, sems):
    width = own.shape[1]
    heads = width // HD
    steps = [(h, min(h + 2, heads)) for h in range(0, heads, 2)]
    copies = []
    for n, (lo, hi) in enumerate(steps):
        cut = pl.ds(lo * HD, (hi - lo) * HD)
        copies.append(pltpu.make_async_copy(weight.at[cut], held.at[cut], sems.at[n]))
        copies[n].start()
    shares = []
    for b in range(2):
        stats = []
        for a in range(8):
            x = [parts[a, r : r + HDR, width:] for r in (0, HDR)]
            x = jnp.concatenate(x, axis=1).astype(F32)
            stats.append(x[3 * b : 3 * b + 1] + x[3 * b + 1 : 3 * b + 2] + x[3 * b + 2 : 3 * b + 3])
        stats = jnp.concatenate(stats, axis=0)
        share = jnp.exp2(stats - jnp.max(stats, axis=0, keepdims=True))
        shares.append((share / jnp.sum(share, axis=0, keepdims=True)).T)
    for h in range(heads):
        for b in range(2):
            x = jnp.zeros((BT, HD), F32)
            for a in range(8):
                part = parts[a, b * BT : (b + 1) * BT, h * HD : (h + 1) * HD].astype(F32)
                x = x + shares[b][h * BT : (h + 1) * BT, a : a + 1] * part
            attended[b * BT : (b + 1) * BT, h * HD : (h + 1) * HD] = x.astype(BF)
    for n, (lo, hi) in enumerate(steps):
        copies[n].wait()
        cut = slice(lo * HD, hi * HD)
        x = jnp.dot(attended[:, cut], held[cut, :], preferred_element_type=F32)
        total[...] = x if n == 0 else total[...] + x
    for by, out in ((1, sibling.at[:, :width]), (3, sibling.at[:, width:]), (2, far), (0, own)):
        at = pl.multiple_of((head[0] ^ by) * width, 128)
        out[...] = total[:, pl.ds(at, width)].astype(out.dtype)


def merge(head, parts, weight):
    tokens, width = parts.shape[1], parts.shape[2] - 128
    return pl.pallas_call(
        merge_kernel,
        out_shape=(
            jax.ShapeDtypeStruct((tokens, width), F32),
            jax.ShapeDtypeStruct((tokens, width), F32),
            jax.ShapeDtypeStruct((tokens, 2 * width), BF),
        ),
        in_specs=[smem(), vmem(), hbm()],
        out_specs=(vmem(),) * 3,
        scratch_shapes=[
            pltpu.VMEM((tokens, width), BF),
            pltpu.VMEM(weight.shape, BF),
            pltpu.VMEM((tokens, weight.shape[1]), F32),
            pltpu.SemaphoreType.DMA((4,)),
        ],
        compiler_params=params(50),
        name="merge",
    )(head, parts, weight)


def local(queries, key_cache, value_cache, out_weight, block_starts, shard_lengths):
    width = queries.shape[1]
    base = (lax.axis_index("seq") * key_cache.shape[0]).astype(jnp.int32).reshape(1)
    head = lax.axis_index("head").astype(jnp.int32).reshape(1)
    message = prepare_queries(block_starts, queries)
    keys = prepare_keys(base, shard_lengths, key_cache)

    gathered = exchange(message)
    k1, v1 = forward((keys, keys)), forward((value_cache, value_cache))
    k2, v2 = forward(k1), forward(v1)
    k3, v3 = forward(k2), forward(v2)
    k4, v4 = swap_even(k3[1]), swap_odd(v3[0])
    kvs = [(keys, value_cache), *zip(k1, v1), *zip(k2, v2), *zip(k3, v3), (k4, v4)]
    state = attend_first(gathered, kvs[:5])
    parts = attend_last(*state, kvs[5:], width)

    parts = exchange(parts)
    own, far, sibling = merge(head, parts, out_weight)
    sibling = swap_head(sibling, 1).astype(F32)
    far = swap_head((far + sibling[:, width:]).astype(BF), 2)
    return (own + sibling[:, :width] + far.astype(F32)).astype(BF)


def solution(mesh):
    placed = (
        P("seq", "head"),
        P("seq", "head"),
        P("seq", "head"),
        P("head", None),
        P("seq"),
        P("seq"),
    )
    return jax.shard_map(
        local, mesh=mesh, in_specs=placed, out_specs=P("seq", "head"), check_vma=False
    )
```

```python
import functools
import math

import jax
import jax.numpy as jnp
import numpy as np
from jax import lax
from jax.experimental import pallas as pl
from jax.experimental.pallas import tpu as pltpu
from jax.sharding import PartitionSpec as P

HD = 128
BT = 32
T = 256
TILES = T // 128
G = 4
R = 256
VR = HD + 16
HDR = 16
SCALE = math.log2(math.e) / math.sqrt(HD)
MASKED = -1e30
FLOOR = -1e29
FAR = 2**30
AXES = ("seq", "head")
MIB = 2**20
BF = jnp.bfloat16
F32 = jnp.float32

GRID = np.arange(256).reshape(4, 2, 8, 2, 2)
CYCLE = [(0, 0), (1, 0), (2, 0), (3, 0), (3, 1), (2, 1), (1, 1), (0, 1)]
SKEW = 0


def key_rings():
    found = []
    for g in range(2):
        for y, x in CYCLE:
            found.append(
                [int(GRID[(y + SKEW * (z // 4)) % 4, x, z, g, 0]) for z in range(8)]
            )
        for z in range(8):
            found.append([int(GRID[y, x, z, g, 1]) for y, x in CYCLE])
    return found


def query_groups():
    found = []
    for g in range(2):
        for z in range(8):
            found.append([int(GRID[y, x, z, g, 0]) for y, x in CYCLE])
        for y, x in CYCLE:
            found.append([int(GRID[y, x, z, g, 1]) for z in range(8)])
    return found


KEY_RINGS = key_rings()
QUERY_GROUPS = query_groups()


def swap_even(x):
    return lax.ppermute(x, AXES, [(r[i], r[i ^ 1]) for r in KEY_RINGS for i in range(8)])


def swap_odd(x):
    pairs = [(r[i], r[(i + 1 if i % 2 else i - 1) % 8]) for r in KEY_RINGS for i in range(8)]
    return lax.ppermute(x, AXES, pairs)


def forward(pair):
    return swap_even(pair[1]), swap_odd(pair[0])


def exchange(x):
    return lax.all_to_all(x, AXES, 0, 0, axis_index_groups=QUERY_GROUPS)


def swap_head(x, by):
    pairs = [(d, (d & ~3) | ((d & 3) ^ by)) for d in range(256)]
    return lax.ppermute(x, AXES, pairs)


def vmem():
    return pl.BlockSpec(memory_space=pltpu.VMEM)


def smem():
    return pl.BlockSpec(memory_space=pltpu.SMEM)


def params(mib):
    return pltpu.CompilerParams(vmem_limit_bytes=mib * MIB)


def hbm():
    return pl.BlockSpec(memory_space=pltpu.HBM)


def run_all(copies):
    for copy in copies:
        copy.start()
    for copy in copies:
        copy.wait()


def queries_kernel(starts, q, message, at_s, wide, sems):
    width = q.shape[1]
    copies = [
        pltpu.make_async_copy(starts, at_s, sems.at[0]),
        pltpu.make_async_copy(q, wide.at[:, pl.ds(0, width)], sems.at[1]),
    ]
    for copy in copies:
        copy.start()
    copies[0].wait()
    row = lax.broadcasted_iota(jnp.int32, (64, 128), 0)
    lane = lax.broadcasted_iota(jnp.int32, (64, 128), 1)
    value = jnp.zeros((64, 128), jnp.int32)
    for e in range(2):
        at = at_s[e]
        value = jnp.where((row == 0) & (lane == e), lax.shift_right_logical(at, 8), value)
        value = jnp.where((row == 1) & (lane == e), at & 255, value)
    wide[:, width:] = value.astype(F32).astype(BF)
    copies[1].wait()
    run_all([pltpu.make_async_copy(wide, message.at[a], sems.at[2 + a]) for a in range(8)])


def prepare_queries(starts, q):
    wide = (q.shape[0], q.shape[1] + 128)
    return pl.pallas_call(
        queries_kernel,
        out_shape=jax.ShapeDtypeStruct((8, *wide), BF),
        in_specs=[hbm(), hbm()],
        out_specs=hbm(),
        scratch_shapes=[
            pltpu.SMEM(starts.shape, jnp.int32),
            pltpu.VMEM(wide, BF),
            pltpu.SemaphoreType.DMA((10,)),
        ],
        compiler_params=params(60),
        name="prepare_queries",
    )(starts, q)


def keys_kernel(base, length, k, out, len_s, sems):
    rows = k.shape[0]
    copies = [
        pltpu.make_async_copy(length, len_s, sems.at[0]),
        pltpu.make_async_copy(k, out.at[pl.ds(0, rows)], sems.at[1]),
    ]
    for copy in copies:
        copy.start()
    copies[0].wait()
    row = lax.broadcasted_iota(jnp.int32, (HDR, HD), 0)
    value = jnp.where(row == 0, lax.shift_right_logical(base[0], 8), base[0] & 255)
    value = jnp.where(row == 2, lax.shift_right_logical(len_s[0], 3), value)
    value = jnp.where(row == 3, len_s[0] & 7, value)
    out[rows:, :] = value.astype(F32).astype(BF)
    copies[1].wait()


def prepare_keys(base, length, k):
    return pl.pallas_call(
        keys_kernel,
        out_shape=jax.ShapeDtypeStruct((k.shape[0] + HDR, HD), BF),
        in_specs=[smem(), hbm(), hbm()],
        out_specs=vmem(),
        scratch_shapes=[
            pltpu.SMEM(length.shape, jnp.int32),
            pltpu.SemaphoreType.DMA((2,)),
        ],
        compiler_params=params(60),
        name="prepare_keys",
    )(base, length, k)


def attend_shards(info, kvs, qb, acc, m, s):
    nb = 16
    rows = kvs[0][1].shape[0]
    tiles = rows // 128
    most = chunks_of(len(kvs) * rows)
    second = most * nb + 4 * G
    heads = []
    for k, _ in kvs:
        h = k[rows:, :].astype(F32)
        base = (h[0:1] * 256.0 + h[1:2]).astype(jnp.int32)
        length = (h[2:3] * 8.0 + h[3:4]).astype(jnp.int32)
        heads.append((base[0, 0], length[0, 0]))

    sub = lax.broadcasted_iota(jnp.int32, (128, 128), 0)
    ones = jnp.ones((VR - HD, 128), BF)
    for c in range(most + 1):
        s.first[c] = FAR
        s.last[c] = -1

    def place(o, k, v, pos):
        c = lax.div(o, TILES)
        r = pl.multiple_of((o - c * TILES) * 128, 128)
        s.keys[c, pl.ds(r, 128), :] = k
        s.values[c, :HD, pl.ds(r, 128)] = v
        s.values[c, HD:, pl.ds(r, 128)] = ones
        s.pos[c, pl.ds(r, 128), :] = pos
        return c

    off = jnp.int32(0)
    for (k, v), (base, length) in zip(kvs, heads, strict=True):
        for t in range(tiles):

            @pl.when(t * 128 < length)
            def _(t=t, off=off, k=k, v=v, base=base, length=length):
                cut = slice(t * 128, (t + 1) * 128)
                pos = jnp.where(sub + t * 128 < length, sub + (base + t * 128), FAR)
                c = place(off + t, k[cut, :], v[cut, :].T, pos)
                s.first[c] = jnp.minimum(s.first[c], base + t * 128)
                end = jnp.where(t * 128 + 128 <= length, base + t * 128 + 127, FAR)
                s.last[c] = jnp.maximum(s.last[c], end)

        off = off + lax.shift_right_logical(length + 127, 7)
    chunks = lax.div(off + TILES - 1, TILES)

    @pl.when(off < chunks * TILES)
    def _():
        c = place(
            off,
            jnp.zeros((128, HD), BF),
            jnp.zeros((HD, 128), BF),
            jnp.full((128, 128), FAR, jnp.int32),
        )
        s.last[c] = FAR

    def per_chunk(c, count):
        lo, hi = s.first[c], s.last[c]

        def per_block(i, count):
            whole, part = count
            at = info[lax.shift_right_logical(i, 1), i & 1]
            is_whole = at >= hi
            is_part = jnp.logical_not(is_whole) & (at + (BT - 1) >= lo)
            s.items[whole] = c * 32 + i
            s.items[second + part] = c * 32 + i
            return whole + is_whole.astype(jnp.int32), part + is_part.astype(jnp.int32)

        whole, part = lax.fori_loop(0, nb, per_block, count, unroll=True)
        for e in range(G - 1):
            s.items[whole + e] = c * 32 + nb
            s.items[second + part + e] = c * 32 + nb
        return lax.div(whole + G - 1, G) * G, lax.div(part + G - 1, G) * G

    whole, part = lax.fori_loop(0, chunks, per_chunk, (jnp.int32(0), jnp.int32(0)))
    for e in range(3 * G):
        s.items[whole + e] = nb
        s.items[second + part + e] = nb

    def score(at, out):
        for e in range(G):
            it = s.items[at + e]
            out[e] = lax.dot_general(
                s.keys[lax.shift_right_logical(it, 5)],
                qb[it & 31],
                (((1,), (1,)), ((), ())),
                preferred_element_type=F32,
            )

    def update(at, score_ref, masked):
        its = [s.items[at + e] for e in range(G)]
        chunk = [lax.shift_right_logical(it, 5) for it in its]
        block = [it & 31 for it in its]
        before = [m[i] for i in block]
        after = []
        for e in range(G):
            if masked:
                i = jnp.minimum(block[e], nb - 1)
                token = lax.broadcasted_iota(jnp.int32, (1, 128), 1) & (BT - 1)
                pos = token + info[lax.shift_right_logical(i, 1), i & 1]
                ok = s.pos[chunk[e]] <= pos
                score_ref[e] = jnp.where(jnp.concatenate([ok, ok], axis=1), score_ref[e], MASKED)
            after.append(
                jnp.maximum(before[e], jnp.max(score_ref[e], axis=0, keepdims=True) * SCALE)
            )
        for e in range(G):
            m[block[e]] = after[e]
        added = []
        for e in range(G):
            p = jnp.exp2(score_ref[e] * SCALE - after[e]).astype(BF)
            added.append(jnp.dot(s.values[chunk[e]], p, preferred_element_type=F32))
        for e in range(G):
            acc[block[e]] = acc[block[e]] * jnp.exp2(before[e] - after[e]) + added[e]

    def run(begin, count, masked):
        @pl.when(count > 0)
        def _():
            score(begin, s.scores_a)

            def body(g, _):
                at = begin + g * (2 * G)
                score(at + G, s.scores_b)
                update(at, s.scores_a, masked)
                score(at + 2 * G, s.scores_a)
                update(at + G, s.scores_b, masked)
                return 0

            lax.fori_loop(0, lax.div(count + 2 * G - 1, 2 * G), body, 0)

    run(0, whole, False)
    run(second, part, True)


def chunks_of(rows):
    return (rows // 128 + TILES - 1) // TILES


class Scratch:
    NAMES = (
        "items",
        "first",
        "last",
        "keys",
        "values",
        "pos",
        "scores_a",
        "scores_b",
    )

    def __init__(self, refs):
        for name, ref in zip(self.NAMES, refs, strict=True):
            setattr(self, name, ref)

    @staticmethod
    def shapes(rows):
        nb, most = 16, chunks_of(rows)
        return [
            pltpu.SMEM((2 * (most * nb + 8 * G),), jnp.int32),
            pltpu.SMEM((most + 1,), jnp.int32),
            pltpu.SMEM((most + 1,), jnp.int32),
            pltpu.VMEM((most + 1, T, HD), BF),
            pltpu.VMEM((most + 1, VR, T), BF),
            pltpu.VMEM((most + 1, T, 128), jnp.int32),
            pltpu.VMEM((G, T, R), F32),
            pltpu.VMEM((G, T, R), F32),
        ]


def pairs(refs):
    return list(zip(refs[0::2], refs[1::2], strict=True))


def begin(queries, info, qb, acc, m, head, sem):
    width = queries.shape[2] - 128
    for a in range(8):
        h = queries[a, :16, width:].astype(F32)
        head[a : a + 1, :] = (h[0:1] * 256.0 + h[1:2]).astype(jnp.int32)
    copy = pltpu.make_async_copy(head, info, sem)
    copy.start()
    heads = width // HD
    for i in range(16):
        for h in range(heads):
            qb[i, h * BT : (h + 1) * BT, :] = queries[
                i // 2, (i % 2) * BT : (i % 2 + 1) * BT, h * HD : (h + 1) * HD
            ]
        qb[i, heads * BT :, :] = jnp.zeros((R - heads * BT, HD), BF)
    qb[16] = jnp.zeros((R, HD), BF)
    acc[...] = jnp.zeros(acc.shape, F32)
    m[...] = jnp.full(m.shape, FLOOR, F32)
    copy.wait()


def cost(shards):
    return pl.CostEstimate(
        flops=shards * 16 * 256 * 640 * 128 * 4, bytes_accessed=MIB, transcendentals=0
    )


def first_kernel(shards, queries, *refs):
    info, qb, acc, m, head, sem, *scratch = refs[2 * shards :]
    begin(queries, info, qb, acc, m, head, sem)
    attend_shards(info, pairs(refs[: 2 * shards]), qb, acc, m, Scratch(scratch))


def attend_first(queries, kvs):
    shards = len(kvs)
    return pl.pallas_call(
        functools.partial(first_kernel, shards),
        out_shape=(
            jax.ShapeDtypeStruct((8, 128), jnp.int32),
            jax.ShapeDtypeStruct((17, R, HD), BF),
            jax.ShapeDtypeStruct((17, VR, R), F32),
            jax.ShapeDtypeStruct((17, 1, R), F32),
        ),
        in_specs=[vmem()] * (1 + 2 * shards),
        out_specs=(smem(), vmem(), vmem(), vmem()),
        scratch_shapes=[pltpu.VMEM((8, 128), jnp.int32), pltpu.SemaphoreType.DMA]
        + Scratch.shapes(shards * kvs[0][1].shape[0]),
        compiler_params=params(16),
        cost_estimate=cost(shards),
        name="attend_first",
    )(queries, *[x for kv in kvs for x in kv])


def next_kernel(shards, info, qb, acc_in, m_in, *refs):
    acc, m, *scratch = refs[2 * shards :]
    attend_shards(info, pairs(refs[: 2 * shards]), qb, acc, m, Scratch(scratch))


def attend_next(info, qb, acc, m, kvs):
    shards = len(kvs)
    acc, m = pl.pallas_call(
        functools.partial(next_kernel, shards),
        out_shape=(
            jax.ShapeDtypeStruct(acc.shape, F32),
            jax.ShapeDtypeStruct(m.shape, F32),
        ),
        in_specs=[smem()] + [vmem()] * (3 + 2 * shards),
        out_specs=(vmem(),) * 2,
        scratch_shapes=Scratch.shapes(shards * kvs[0][1].shape[0]),
        input_output_aliases={2: 0, 3: 1},
        compiler_params=params(16),
        cost_estimate=cost(shards),
        name="attend_next",
    )(info, qb, acc, m, *[x for kv in kvs for x in kv])
    return info, qb, acc, m


def last_kernel(shards, info, qb, acc_in, m_in, *refs):
    out, acc, m, *scratch = refs[2 * shards :]
    attend_shards(info, pairs(refs[: 2 * shards]), qb, acc, m, Scratch(scratch))
    conclude(acc, m, out)


def attend_last(info, qb, acc, m, kvs, width):
    shards = len(kvs)
    out, _, _ = pl.pallas_call(
        functools.partial(last_kernel, shards),
        out_shape=(
            jax.ShapeDtypeStruct((8, 2 * BT, width + 128), BF),
            jax.ShapeDtypeStruct(acc.shape, F32),
            jax.ShapeDtypeStruct(m.shape, F32),
        ),
        in_specs=[smem()] + [vmem()] * (3 + 2 * shards),
        out_specs=(vmem(),) * 3,
        scratch_shapes=Scratch.shapes(shards * kvs[0][1].shape[0]),
        input_output_aliases={2: 1, 3: 2},
        compiler_params=params(16),
        cost_estimate=cost(shards),
        name="attend_last",
    )(info, qb, acc, m, *[x for kv in kvs for x in kv])
    return out


def whole_kernel(shards, queries, *refs):
    out, info, qb, acc, m, head, sem, *scratch = refs[2 * shards :]
    begin(queries, info, qb, acc, m, head, sem)
    attend_shards(info, pairs(refs[: 2 * shards]), qb, acc, m, Scratch(scratch))
    conclude(acc, m, out)


def attend(queries, kvs):
    shards = len(kvs)
    return pl.pallas_call(
        functools.partial(whole_kernel, shards),
        out_shape=jax.ShapeDtypeStruct(queries.shape, BF),
        in_specs=[vmem()] * (1 + 2 * shards),
        out_specs=vmem(),
        scratch_shapes=[
            pltpu.SMEM((8, 128), jnp.int32),
            pltpu.VMEM((17, R, HD), BF),
            pltpu.VMEM((17, VR, R), F32),
            pltpu.VMEM((17, 1, R), F32),
            pltpu.VMEM((8, 128), jnp.int32),
            pltpu.SemaphoreType.DMA,
        ]
        + Scratch.shapes(shards * kvs[0][1].shape[0]),
        compiler_params=params(24),
        cost_estimate=cost(shards),
        name="attend",
    )(queries, *[x for kv in kvs for x in kv])


def conclude(acc, m, out):
    heads = out.shape[2] // HD - 1

    def finish(a, _):
        stats = []
        for b in range(2):
            i = 2 * a + b
            total = acc[i, HD : HD + 1, :]
            some = total > 0.0
            o = acc[i, :HD, :] * jnp.where(some, 1.0 / jnp.where(some, total, 1.0), 0.0)
            o = o.astype(BF).T
            for h in range(heads):
                out[a, b * BT : (b + 1) * BT, h * HD : (h + 1) * HD] = o[h * BT : (h + 1) * BT]
            lse = jnp.where(some, m[i] + jnp.log2(jnp.where(some, total, 1.0)), MASKED)
            for _ in range(3):
                part = lse.astype(BF).astype(F32)
                stats.append(part)
                lse = lse - part
        stats = jnp.concatenate(stats + [jnp.zeros((HDR - 6, R), F32)], axis=0).astype(BF)
        out[a, :HDR, heads * HD :] = stats[:, :128]
        out[a, HDR : 2 * HDR, heads * HD :] = stats[:, 128:]
        out[a, 2 * HDR :, heads * HD :] = jnp.zeros((2 * BT - 2 * HDR, 128), BF)
        return 0

    lax.fori_loop(0, 8, finish, 0, unroll=4)


def merge_kernel(head, parts, weight, own, far, sibling, attended, held, total, sems):
    width = own.shape[1]
    heads = width // HD
    steps = [(h, min(h + 2, heads)) for h in range(0, heads, 2)]
    copies = []
    for n, (lo, hi) in enumerate(steps):
        cut = pl.ds(lo * HD, (hi - lo) * HD)
        copies.append(pltpu.make_async_copy(weight.at[cut], held.at[cut], sems.at[n]))
        copies[n].start()
    shares = []
    for b in range(2):
        stats = []
        for a in range(8):
            x = [parts[a, r : r + HDR, width:] for r in (0, HDR)]
            x = jnp.concatenate(x, axis=1).astype(F32)
            stats.append(x[3 * b : 3 * b + 1] + x[3 * b + 1 : 3 * b + 2] + x[3 * b + 2 : 3 * b + 3])
        stats = jnp.concatenate(stats, axis=0)
        share = jnp.exp2(stats - jnp.max(stats, axis=0, keepdims=True))
        shares.append((share / jnp.sum(share, axis=0, keepdims=True)).T)
    for h in range(heads):
        for b in range(2):
            x = jnp.zeros((BT, HD), F32)
            for a in range(8):
                part = parts[a, b * BT : (b + 1) * BT, h * HD : (h + 1) * HD].astype(F32)
                x = x + shares[b][h * BT : (h + 1) * BT, a : a + 1] * part
            attended[b * BT : (b + 1) * BT, h * HD : (h + 1) * HD] = x.astype(BF)
    for n, (lo, hi) in enumerate(steps):
        copies[n].wait()
        cut = slice(lo * HD, hi * HD)
        x = jnp.dot(attended[:, cut], held[cut, :], preferred_element_type=F32)
        total[...] = x if n == 0 else total[...] + x
    for by, out in ((1, sibling.at[:, :width]), (3, sibling.at[:, width:]), (2, far), (0, own)):
        at = pl.multiple_of((head[0] ^ by) * width, 128)
        out[...] = total[:, pl.ds(at, width)].astype(out.dtype)


def merge(head, parts, weight):
    tokens, width = parts.shape[1], parts.shape[2] - 128
    return pl.pallas_call(
        merge_kernel,
        out_shape=(
            jax.ShapeDtypeStruct((tokens, width), F32),
            jax.ShapeDtypeStruct((tokens, width), F32),
            jax.ShapeDtypeStruct((tokens, 2 * width), BF),
        ),
        in_specs=[smem(), vmem(), hbm()],
        out_specs=(vmem(),) * 3,
        scratch_shapes=[
            pltpu.VMEM((tokens, width), BF),
            pltpu.VMEM(weight.shape, BF),
            pltpu.VMEM((tokens, weight.shape[1]), F32),
            pltpu.SemaphoreType.DMA((4,)),
        ],
        compiler_params=params(50),
        name="merge",
    )(head, parts, weight)


def local(queries, key_cache, value_cache, out_weight, block_starts, shard_lengths):
    width = queries.shape[1]
    base = (lax.axis_index("seq") * key_cache.shape[0]).astype(jnp.int32).reshape(1)
    head = lax.axis_index("head").astype(jnp.int32).reshape(1)
    message = prepare_queries(block_starts, queries)
    keys = prepare_keys(base, shard_lengths, key_cache)

    gathered = exchange(message)
    k1, v1 = forward((keys, keys)), forward((value_cache, value_cache))
    k2, v2 = forward(k1), forward(v1)
    k3, v3 = forward(k2), forward(v2)
    info, qb, acc, m = attend_first(gathered, [(k1[0], v1[0])])
    k3, v3, acc = lax.optimization_barrier((k3, v3, acc))
    k4, v4 = swap_even(k3[1]), swap_odd(v3[0])
    kvs = [(k1[1], v1[1]), (keys, value_cache), *zip(k2, v2)]
    state = attend_next(info, qb, acc, m, kvs)
    parts = attend_last(*state, [*zip(k3, v3), (k4, v4)], width)

    parts = exchange(parts)
    own, far, sibling = merge(head, parts, out_weight)
    sibling = swap_head(sibling, 1).astype(F32)
    far = swap_head((far + sibling[:, width:]).astype(BF), 2)
    return (own + sibling[:, :width] + far.astype(F32)).astype(BF)


def solution(mesh):
    placed = (
        P("seq", "head"),
        P("seq", "head"),
        P("seq", "head"),
        P("head", None),
        P("seq"),
        P("seq"),
    )
    return jax.shard_map(
        local, mesh=mesh, in_specs=placed, out_specs=P("seq", "head"), check_vma=False
    )
```
